1024 devices in a mesh: pipe: 8 (over y_lo, core), expert: 32 (over y_hi, z), dp: 4 (over x).
Axes of the slice: x: 4, y: 8 (y_hi: 2, y_lo: 4; y = y_hi * 4 + y_lo), z: 16, core: 2. Of those that a mesh axis runs over, the one named last changes fastest.
Arguments:
- stream: bfloat16 [8, 2, 2048, 7168], P('pipe', None, 'expert', 'dp'), may hold values from -11 to 11
- routes: int32 [8, 2, 2048, 8], P('pipe', None, 'expert'), may hold values from 0 to 255, as said below
- gates: float32 [8, 2, 2048, 8], P('pipe', None, 'expert'), may hold values from 0.2 to 1
- expert_hidden: bfloat16 [8, 2, 256, 16384], P('pipe', None, None, 'expert'), may hold values from -6 to 6
- down_weight: bfloat16 [8, 16384, 7168], P('pipe', 'expert', 'dp'), may hold values from -0.1875 to 0.1875
- norm_gain: float32 [8, 7168], P(None, 'dp'), may hold values from 0.5 to 1.5
Outputs:
- next_stream: bfloat16 [8, 2, 2048, 7168], P('pipe', None, 'expert', 'dp')
- next_normed: bfloat16 [8, 2, 2048, 7168], P('pipe', None, 'expert', 'dp')
The draws below stay inside these ranges and needn't reach their ends.
Inputs may be any that keep to these rules, and one draw needn't show every extreme that they name: `routes`: each row names 8 different experts. For every expert below 16, at most 8 of the 64 rows of one aligned block of a micro-batch and section name it, and in each micro-batch of each section some expert below 16 is named by exactly 8 rows of every block.
All inputs are finite; a program needn't handle non-finite values.
Results may differ from the reference program's by a relative error of at most 0.0048.
Values may be sent and summed in bfloat16 or wider, within the bound.
No kernel may reach another device: no remote copies, remote signals or barrier semaphores. Data moves between devices by JAX's collectives and lax.ppermute only.
A program may use at most 32 MiB of HBM per device.

```python
import math
import jax
import jax.numpy as jnp
from jax import lax

D = 7168
EXPERTS_ALL = 256
TOPK = 8
FH = 1024
MOST = 8
TOK_DEV = 64
SECTIONS = 8
WINDOW = 16
TOKENS = 2048
SLOTS = 256


def draw_routes(key, part):
    key = jax.random.fold_in(key, 5)
    keys = jax.random.split(key, 5)
    groups = SECTIONS * 2
    blocks = TOKENS // TOK_DEV
    layers = (WINDOW + TOPK - 1) // TOPK
    hottest = jax.random.randint(keys[0], (groups, 1, 1), 0, WINDOW)
    loads = jax.random.randint(keys[1], (groups, blocks, WINDOW), 0, MOST + 1)
    loads = jnp.where(jnp.arange(WINDOW)[None, None, :] == hottest, MOST, loads)
    scores = jax.random.randint(keys[2], (groups, blocks, TOPK, TOK_DEV), 0, 1048576) * TOK_DEV + jnp.arange(TOK_DEV)
    ranks = jnp.argsort(jnp.argsort(scores, axis=-1), axis=-1)
    residue = jnp.arange(TOPK)[None, None, :, None]
    level = ranks // MOST
    expert = residue + TOPK * level
    usable = (level < layers) & (expert < WINDOW)
    spread_loads = jnp.broadcast_to(loads[:, :, None, :], (groups, blocks, TOPK, WINDOW))
    capped = jnp.take_along_axis(spread_loads, jnp.minimum(expert, WINDOW - 1), axis=3)
    usable = usable & (ranks % MOST < capped)
    outside = residue + TOPK * jax.random.randint(keys[3], (groups, blocks, TOPK, TOK_DEV), layers, EXPERTS_ALL // TOPK)
    chosen = jnp.swapaxes(jnp.where(usable, expert, outside), 2, 3)
    shuffle = jax.random.randint(keys[4], chosen.shape, 0, 1048576) * TOPK + jnp.arange(TOPK)
    chosen = jnp.take_along_axis(chosen, jnp.argsort(shuffle, axis=-1), axis=-1)
    return chosen.reshape(SECTIONS, 2, TOKENS, TOPK).astype(jnp.int32)


def draw_stream(key, part):
    key = jax.random.fold_in(key, 9)
    key_base, key_rows = jax.random.split(key, 2)
    shape = (SECTIONS, 2, TOKENS, D)
    position = jnp.arange(D, dtype=jnp.float32) / D
    base = jnp.clip(jax.random.normal(key_base, shape, jnp.float32), -3.0, 3.0)
    scales = jnp.exp(jax.random.uniform(key_rows, (SECTIONS, 2, TOKENS, 1), jnp.float32, math.log(0.6), math.log(1.8)))
    columns = 0.2 * jnp.exp(position * math.log(10.0))
    return (base * scales * columns).astype(jnp.bfloat16)


def block_scale(rng, dims, cuts, smallest, high):
    factor_of = 1.0
    for dim, blocks in cuts:
        draws = jax.random.uniform(jax.random.fold_in(jax.random.fold_in(rng, 6), dim), (blocks,), jnp.float32, smallest / len(cuts), high / len(cuts))
        factor_of = factor_of * jnp.repeat(jnp.exp(draws), dims[dim] // blocks).reshape((-1,) + (1,) * (len(dims) - 1 - dim))
    return factor_of


def gaussian(rng, dims, width, reach, cuts=(), kind=jnp.bfloat16):
    drawn = width * jax.random.normal(rng, dims, jnp.float32)
    if cuts:
        drawn = drawn * block_scale(rng, dims, cuts, -0.22, 0.18)
    return jnp.clip(drawn, -reach, reach).astype(kind)


def setup_inputs(seed: int = 0) -> dict:
    key_list = jax.random.split(jax.random.key(seed), 7)
    return {
        "stream": draw_stream(jax.random.fold_in(key_list[6], 71), 0),
        "routes": draw_routes(jax.random.fold_in(key_list[6], 71), 0),
        "gates": jnp.clip(0.2 + 0.8 * jax.random.uniform(key_list[2], (SECTIONS, 2, TOKENS, TOPK), jnp.float32) ** block_scale(key_list[2], (SECTIONS, 2, TOKENS, TOPK), ((0, 8), (2, 32)), -0.2, 0.2), 0.2, 1.0),
        "expert_hidden": gaussian(key_list[3], (SECTIONS, 2, SLOTS, WINDOW * FH), 1.0, 6.0, ((0, 8), (3, 32))),
        "down_weight": gaussian(key_list[4], (SECTIONS, WINDOW * FH, D), FH ** -0.5, 0.1875, ((0, 8), (1, 32), (2, 4))),
        "norm_gain": jnp.clip(1.0 + 0.1 * jax.random.normal(key_list[5], (SECTIONS, D), jnp.float32), 0.5, 1.5),
    }


def routing_tables(routes, gates):
    experts = jnp.arange(WINDOW, dtype=jnp.int32)
    matches = routes[..., None] == experts
    is_routed = jnp.any(matches, axis=2).astype(jnp.int32)
    blocked = is_routed.reshape(2, TOKENS // TOK_DEV, TOK_DEV, WINDOW)
    slot_rank = (jnp.cumsum(blocked, axis=2) - 1).reshape(is_routed.shape)
    gate_sum = lax.optimization_barrier(jnp.sum(jnp.where(matches, gates[..., None], jnp.float32(0.0)), axis=2))
    source = jnp.arange(TOKENS, dtype=jnp.int32) // TOK_DEV
    slot_index = (source[None, :, None] * MOST + jnp.maximum(slot_rank, 0)).astype(jnp.int32)
    row_weight = gate_sum * is_routed.astype(jnp.float32)
    return (slot_index, row_weight)

def one_section(inputs):
    residual, routes, gates, hidden_all, weight_all, gain = inputs
    slot_index, row_weight = routing_tables(routes, gates)
    half = FH // 2

    def one_block(total, device):
        offset = (device * half).astype(jnp.int32)
        hidden = lax.dynamic_slice_in_dim(hidden_all, offset, half, 2).astype(jnp.float32)
        rows = lax.dynamic_slice_in_dim(weight_all, offset, half, 0).astype(jnp.float32)
        partial_value = jnp.einsum('msf,fd->msd', hidden, rows, precision=lax.Precision.HIGHEST)
        partial_value = lax.optimization_barrier(partial_value.astype(jnp.bfloat16)).astype(jnp.float32)
        expert = (device // 2).astype(jnp.int32)
        chosen_slots = jnp.take(slot_index, expert, axis=2)
        chosen_weight = jnp.take(row_weight, expert, axis=2)
        picked = jnp.take_along_axis(partial_value, chosen_slots[..., None], axis=1)
        return (total + chosen_weight[..., None] * picked, None)
    start_total = jnp.zeros((2, TOKENS, D), jnp.float32)
    combined, _ = lax.scan(one_block, start_total, jnp.arange(2 * WINDOW, dtype=jnp.int32))
    layer_out = (residual.astype(jnp.float32) + combined).astype(jnp.bfloat16)
    floats = layer_out.astype(jnp.float32)
    mean_square = lax.optimization_barrier(jnp.sum(floats * floats, axis=-1, keepdims=True)) / D
    normed = (floats * lax.rsqrt(mean_square + 1e-06) * gain).astype(jnp.bfloat16)
    return (layer_out, normed)

def hand_off(values):
    blank_rows = jnp.zeros((1, TOKENS, D), jnp.bfloat16)
    forward_rows = jnp.concatenate([blank_rows, values[:-1, 0]], axis=0)
    backward_rows = jnp.concatenate([values[1:, 1], blank_rows], axis=0)
    return jnp.stack([forward_rows, backward_rows], axis=1)

def reference(stream, routes, gates, expert_hidden, down_weight, norm_gain):
    streams, normed_all = lax.map(one_section, (stream, routes, gates, expert_hidden, down_weight, norm_gain))
    return (hand_off(streams), hand_off(normed_all))
```

```python
import jax
import jax.numpy as jnp
from jax import lax
from jax.sharding import PartitionSpec as P

D = 7168
EPSILON = 1e-06
CAPACITY = 8


def shifted(block, distance):
    sections = range(lax.axis_size("pipe"))
    route = [(i - distance, i) for i in sections if i - distance in sections]
    return lax.ppermute(block, "pipe", route)


def shifted_to_partner(block, distance):
    sections, blocks = lax.axis_size("pipe"), lax.axis_size("expert")
    route = [
        (i * blocks + j, (i + distance) * blocks + (j ^ 1))
        for i in range(sections)
        if 0 <= i + distance < sections
        for j in range(blocks)
    ]
    return lax.ppermute(block, ("pipe", "expert"), route)


def route_weights(routes, gates, experts):
    matches = routes[:, :, None] == jnp.arange(experts, dtype=jnp.int32)
    is_routed = jnp.any(matches, axis=1)
    tokens = routes.shape[0]
    earlier = jnp.tril(jnp.ones((tokens, tokens), jnp.bfloat16), -1)
    rank = jnp.dot(earlier, is_routed.astype(jnp.bfloat16), preferred_element_type=jnp.float32)
    gate_sum = jnp.sum(jnp.where(matches, gates[:, :, None], 0.0), axis=1)
    slots = jnp.arange(CAPACITY, dtype=jnp.float32)
    chosen = is_routed[..., None] & (rank[..., None] == slots)
    return jnp.where(chosen, gate_sum[..., None], 0.0).reshape(tokens, experts * CAPACITY)


def per_device(stream, routes, gates, expert_hidden, down_weight, norm_gain):
    blocks = lax.axis_size("expert")
    experts = blocks // 2
    parity = lax.axis_index("expert") % 2
    section = lax.axis_index("pipe")
    sections = lax.axis_size("pipe")
    tokens, columns = stream.shape[2:]
    halves = [[j for j in range(blocks) if j % 2 == q] for q in range(2)]
    hidden = expert_hidden[0].reshape(2, experts, 2, CAPACITY, -1)
    kept = lax.dynamic_index_in_dim(hidden, parity, 2, keepdims=False).reshape(2, experts * CAPACITY, -1)
    sent = lax.dynamic_index_in_dim(hidden, 1 - parity, 2, keepdims=False).reshape(2, experts * CAPACITY, -1)

    def project(rows):
        return jnp.dot(rows, down_weight[0], preferred_element_type=jnp.float32).astype(jnp.bfloat16)

    sums = []
    for m, distance in enumerate((1, -1)):
        theirs = shifted_to_partner(project(sent[m]), distance)
        own = shifted(project(kept[m]), distance)
        total = (theirs.astype(jnp.float32) + own.astype(jnp.float32)).astype(jnp.bfloat16)
        sums.append(total.reshape(experts, CAPACITY, columns))
    exchanged = lax.all_to_all(
        jnp.stack(sums, axis=1), "expert", 0, 0, axis_index_groups=halves, tiled=True
    )
    outs = []
    for m, distance in enumerate((1, -1)):
        weights = route_weights(routes[0, m], gates[0, m], experts)
        high = weights.astype(jnp.bfloat16)
        low = (weights - high.astype(jnp.float32)).astype(jnp.bfloat16)
        side = shifted(jnp.concatenate([stream[0, m], high, low], axis=1), distance)
        received = exchanged[:, m].reshape(experts * CAPACITY, columns)
        residual = side[:, :columns].astype(jnp.float32)
        high, low = jnp.split(side[:, columns:], 2, axis=1)
        combined = jnp.dot(high, received, preferred_element_type=jnp.float32) + jnp.dot(
            low, received, preferred_element_type=jnp.float32
        )
        layer_out = (residual + combined).astype(jnp.bfloat16)
        floats = layer_out.astype(jnp.float32)
        totals = lax.psum(jnp.sum(floats * floats, axis=-1), "dp")
        gain = lax.dynamic_index_in_dim(norm_gain, jnp.clip(section - distance, 0, sections - 1), 0, keepdims=False)
        normed = (floats * lax.rsqrt(totals / D + EPSILON)[:, None] * gain).astype(jnp.bfloat16)
        outs.append((layer_out, normed))
    next_stream = jnp.stack([outs[0][0], outs[1][0]], axis=0)[None]
    next_normed = jnp.stack([outs[0][1], outs[1][1]], axis=0)[None]
    return (next_stream, next_normed)


def solution(mesh):
    in_specs = (
        P("pipe", None, "expert", "dp"),
        P("pipe", None, "expert", None),
        P("pipe", None, "expert", None),
        P("pipe", None, None, "expert"),
        P("pipe", "expert", "dp"),
        P(None, "dp"),
    )
    out_specs = (P("pipe", None, "expert", "dp"), P("pipe", None, "expert", "dp"))
    return jax.shard_map(
        per_device, mesh=mesh, in_specs=in_specs, out_specs=out_specs, check_vma=False
    )
```

```python
import jax
import jax.numpy as jnp
from jax import lax
from jax.experimental import pallas as pl
from jax.experimental.pallas import tpu as pltpu
from jax.sharding import PartitionSpec as P

D = 7168
EPSILON = 1e-06
CAPACITY = 8


def shifted(block, distance):
    sections = range(lax.axis_size("pipe"))
    route = [(i - distance, i) for i in sections if i - distance in sections]
    return lax.ppermute(block, "pipe", route)


def shifted_to_partner(block, distance):
    sections, blocks = lax.axis_size("pipe"), lax.axis_size("expert")
    route = [
        (i * blocks + j, (i + distance) * blocks + (j ^ 1))
        for i in range(sections)
        if 0 <= i + distance < sections
        for j in range(blocks)
    ]
    return lax.ppermute(block, ("pipe", "expert"), route)


def route_weights(routes, gates, experts, m):
    tokens = routes.shape[0]
    column = jnp.arange(experts * 2 * CAPACITY, dtype=jnp.int32)
    matches = routes[:, :, None] == column // (2 * CAPACITY)
    is_routed = jnp.any(matches, axis=1)
    earlier = jnp.tril(jnp.ones((tokens, tokens), jnp.bfloat16), -1)
    rank = jnp.dot(earlier, is_routed.astype(jnp.bfloat16), preferred_element_type=jnp.float32)
    gate_sum = jnp.sum(jnp.where(matches, gates[:, :, None], 0.0), axis=1)
    slot = column % (2 * CAPACITY) - m * CAPACITY
    chosen = is_routed & (rank == slot.astype(jnp.float32)) & (slot >= 0)
    return jnp.where(chosen, gate_sum, 0.0)


def combine_kernel(received_ref, side0_ref, side1_ref, out_ref, squares_ref):
    received = received_ref[...]
    slots, columns = received.shape
    for m, side_ref in enumerate((side0_ref, side1_ref)):
        high = side_ref[:, columns : columns + slots]
        low = side_ref[:, columns + slots :]
        combined = jnp.dot(high, received, preferred_element_type=jnp.float32)
        combined += jnp.dot(low, received, preferred_element_type=jnp.float32)
        layer_out = (side_ref[:, :columns].astype(jnp.float32) + combined).astype(jnp.bfloat16)
        out_ref[0, m] = layer_out
        floats = layer_out.astype(jnp.float32)
        squares_ref[m] = jnp.sum(floats * floats, axis=1, keepdims=True)


def combine(received, sides, tokens):
    slots, columns = received.shape
    return pl.pallas_call(
        combine_kernel,
        out_shape=(
            jax.ShapeDtypeStruct((1, 2, tokens, columns), jnp.bfloat16),
            jax.ShapeDtypeStruct((2, tokens, 1), jnp.float32),
        ),
        cost_estimate=pl.CostEstimate(
            flops=8 * tokens * slots * columns, bytes_accessed=2 * slots * columns, transcendentals=0
        ),
        compiler_params=pltpu.CompilerParams(vmem_limit_bytes=16 << 20),
    )(received, *sides)


def per_device(stream, routes, gates, expert_hidden, down_weight, norm_gain):
    blocks = lax.axis_size("expert")
    experts = blocks // 2
    parity = lax.axis_index("expert") % 2
    section = lax.axis_index("pipe")
    sections = lax.axis_size("pipe")
    tokens, columns = stream.shape[2:]
    halves = [[j for j in range(blocks) if j % 2 == q] for q in range(2)]
    hidden = expert_hidden[0].reshape(2, experts, 2, CAPACITY, -1)
    kept = lax.dynamic_index_in_dim(hidden, parity, 2, keepdims=False).reshape(2, experts * CAPACITY, -1)
    sent = lax.dynamic_index_in_dim(hidden, 1 - parity, 2, keepdims=False).reshape(2, experts * CAPACITY, -1)

    def project(rows):
        return jnp.dot(rows, down_weight[0], preferred_element_type=jnp.float32).astype(jnp.bfloat16)

    sums = []
    for m, distance in enumerate((1, -1)):
        theirs = shifted_to_partner(project(sent[m]), distance)
        own = shifted(project(kept[m]), distance)
        total = (theirs.astype(jnp.float32) + own.astype(jnp.float32)).astype(jnp.bfloat16)
        sums.append(total.reshape(experts, CAPACITY, columns))
    exchanged = lax.all_to_all(
        jnp.stack(sums, axis=1), "expert", 0, 0, axis_index_groups=halves, tiled=True
    )
    sides = []
    for m, distance in enumerate((1, -1)):
        weights = route_weights(routes[0, m], gates[0, m], experts, m)
        high = weights.astype(jnp.bfloat16)
        low = (weights - high.astype(jnp.float32)).astype(jnp.bfloat16)
        sides.append(shifted(jnp.concatenate([stream[0, m], high, low], axis=1), distance))
    next_stream, squares = combine(exchanged.reshape(experts * 2 * CAPACITY, columns), sides, tokens)
    totals = lax.psum(squares.reshape(2, tokens), "dp")
    factor = lax.rsqrt(totals / D + EPSILON)
    gains = jnp.stack(
        [
            lax.dynamic_index_in_dim(norm_gain, jnp.clip(section - distance, 0, sections - 1), 0, keepdims=False)
            for distance in (1, -1)
        ]
    )
    normed = next_stream.astype(jnp.float32) * factor[None, :, :, None] * gains[None, :, None, :]
    return (next_stream, normed.astype(jnp.bfloat16))


def solution(mesh):
    in_specs = (
        P("pipe", None, "expert", "dp"),
        P("pipe", None, "expert", None),
        P("pipe", None, "expert", None),
        P("pipe", None, None, "expert"),
        P("pipe", "expert", "dp"),
        P(None, "dp"),
    )
    out_specs = (P("pipe", None, "expert", "dp"), P("pipe", None, "expert", "dp"))
    return jax.shard_map(
        per_device, mesh=mesh, in_specs=in_specs, out_specs=out_specs, check_vma=False
    )
```

```python
import jax
import jax.numpy as jnp
from jax import lax
from jax.experimental import pallas as pl
from jax.experimental.pallas import tpu as pltpu
from jax.sharding import PartitionSpec as P

D = 7168
EPSILON = 1e-06
CAPACITY = 8


def shifted(block, distance):
    sections = range(lax.axis_size("pipe"))
    route = [(i - distance, i) for i in sections if i - distance in sections]
    return lax.ppermute(block, "pipe", route)


def shifted_to_partner(block, distance):
    sections, blocks = lax.axis_size("pipe"), lax.axis_size("expert")
    route = [
        (i * blocks + j, (i + distance) * blocks + (j ^ 1))
        for i in range(sections)
        if 0 <= i + distance < sections
        for j in range(blocks)
    ]
    return lax.ppermute(block, ("pipe", "expert"), route)


def route_weights(routes, gates, experts, m):
    tokens = routes.shape[0]
    column = jnp.arange(experts * 2 * CAPACITY, dtype=jnp.int32)
    matches = routes[:, :, None] == column // (2 * CAPACITY)
    is_routed = jnp.any(matches, axis=1)
    earlier = jnp.tril(jnp.ones((tokens, tokens), jnp.bfloat16), -1)
    rank = jnp.dot(earlier, is_routed.astype(jnp.bfloat16), preferred_element_type=jnp.float32)
    gate_sum = jnp.sum(jnp.where(matches, gates[:, :, None], 0.0), axis=1)
    slot = column % (2 * CAPACITY) - m * CAPACITY
    chosen = is_routed & (rank == slot.astype(jnp.float32)) & (slot >= 0)
    return jnp.where(chosen, gate_sum, 0.0)


def on_diagonal(size):
    return lax.broadcasted_iota(jnp.int32, (size, size), 0) == lax.broadcasted_iota(jnp.int32, (size, size), 1)


def combine_kernel(received_ref, side0_ref, side1_ref, out_ref, copy_ref, squares_ref):
    received = received_ref[...]
    slots, columns = received.shape
    for m, side_ref in enumerate((side0_ref, side1_ref)):
        high = side_ref[:, columns : columns + slots]
        low = side_ref[:, columns + slots :]
        combined = jnp.dot(high, received, preferred_element_type=jnp.float32)
        combined += jnp.dot(low, received, preferred_element_type=jnp.float32)
        layer_out = (side_ref[:, :columns].astype(jnp.float32) + combined).astype(jnp.bfloat16)
        out_ref[0, m] = layer_out
        copy_ref[m] = layer_out
        floats = layer_out.astype(jnp.float32)
        total = jnp.sum(floats * floats, axis=1, keepdims=True)
        squares_ref[m : m + 1] = jnp.sum(jnp.where(on_diagonal(floats.shape[0]), total, 0.0), axis=0, keepdims=True)


def combine(received, sides, tokens):
    slots, columns = received.shape
    return pl.pallas_call(
        combine_kernel,
        out_shape=(
            jax.ShapeDtypeStruct((1, 2, tokens, columns), jnp.bfloat16),
            jax.ShapeDtypeStruct((2, tokens, columns), jnp.bfloat16),
            jax.ShapeDtypeStruct((2, tokens), jnp.float32),
        ),
        cost_estimate=pl.CostEstimate(
            flops=8 * tokens * slots * columns, bytes_accessed=2 * slots * columns, transcendentals=0
        ),
        compiler_params=pltpu.CompilerParams(vmem_limit_bytes=8 << 20),
    )(received, *sides)


def norm_kernel(rows_ref, totals_ref, gains_ref, out_ref):
    tokens, columns = rows_ref.shape[1:]
    totals = jnp.sum(totals_ref[...], axis=0)
    for m in range(2):
        total = jnp.sum(jnp.where(on_diagonal(tokens), totals[m : m + 1], 0.0), axis=1, keepdims=True)
        factor = lax.rsqrt(total / D + EPSILON)
        normed = rows_ref[m].astype(jnp.float32) * factor * gains_ref[m : m + 1]
        out_ref[0, m] = normed.astype(jnp.bfloat16)


def normalize(rows, totals, gains):
    return pl.pallas_call(
        norm_kernel,
        out_shape=jax.ShapeDtypeStruct((1, *rows.shape), jnp.bfloat16),
        cost_estimate=pl.CostEstimate(flops=4 * rows.size, bytes_accessed=4 * rows.size, transcendentals=0),
        compiler_params=pltpu.CompilerParams(vmem_limit_bytes=8 << 20),
    )(rows, totals, gains)


def per_device(stream, routes, gates, expert_hidden, down_weight, norm_gain):
    blocks = lax.axis_size("expert")
    experts = blocks // 2
    parity = lax.axis_index("expert") % 2
    section = lax.axis_index("pipe")
    sections = lax.axis_size("pipe")
    tokens, columns = stream.shape[2:]
    halves = [[j for j in range(blocks) if j % 2 == q] for q in range(2)]
    hidden = expert_hidden[0].reshape(2, experts, 2, CAPACITY, -1)
    kept = lax.dynamic_index_in_dim(hidden, parity, 2, keepdims=False).reshape(2, experts * CAPACITY, -1)
    sent = lax.dynamic_index_in_dim(hidden, 1 - parity, 2, keepdims=False).reshape(2, experts * CAPACITY, -1)

    def project(rows):
        return jnp.dot(rows, down_weight[0], preferred_element_type=jnp.float32).astype(jnp.bfloat16)

    sums = []
    for m, distance in enumerate((1, -1)):
        theirs = shifted_to_partner(project(sent[m]), distance)
        own = shifted(project(kept[m]), distance)
        total = (theirs.astype(jnp.float32) + own.astype(jnp.float32)).astype(jnp.bfloat16)
        sums.append(total.reshape(experts, CAPACITY, columns))
    exchanged = lax.all_to_all(
        jnp.stack(sums, axis=1), "expert", 0, 0, axis_index_groups=halves, tiled=True
    )
    sides = []
    for m, distance in enumerate((1, -1)):
        weights = route_weights(routes[0, m], gates[0, m], experts, m)
        high = weights.astype(jnp.bfloat16)
        low = (weights - high.astype(jnp.float32)).astype(jnp.bfloat16)
        sides.append(shifted(jnp.concatenate([stream[0, m], high, low], axis=1), distance))
    received = exchanged.reshape(experts * 2 * CAPACITY, columns)
    next_stream, rows, squares = combine(received, sides, tokens)
    totals = lax.all_gather(squares, "dp")
    gains = jnp.stack(
        [
            lax.dynamic_index_in_dim(norm_gain, jnp.clip(section - distance, 0, sections - 1), 0, keepdims=False)
            for distance in (1, -1)
        ]
    )
    return (next_stream, normalize(rows, totals, gains))


def solution(mesh):
    in_specs = (
        P("pipe", None, "expert", "dp"),
        P("pipe", None, "expert", None),
        P("pipe", None, "expert", None),
        P("pipe", None, None, "expert"),
        P("pipe", "expert", "dp"),
        P(None, "dp"),
    )
    out_specs = (P("pipe", None, "expert", "dp"), P("pipe", None, "expert", "dp"))
    return jax.shard_map(
        per_device, mesh=mesh, in_specs=in_specs, out_specs=out_specs, check_vma=False
    )
```

```python
import jax
import jax.numpy as jnp
from jax import lax
from jax.experimental import pallas as pl
from jax.experimental.pallas import tpu as pltpu
from jax.sharding import PartitionSpec as P

D = 7168
EPSILON = 1e-06
CAPACITY = 8


def shifted(block, distance):
    sections = range(lax.axis_size("pipe"))
    route = [(i - distance, i) for i in sections if i - distance in sections]
    return lax.ppermute(block, "pipe", route)


def shifted_to_partner(block, distance):
    sections, blocks = lax.axis_size("pipe"), lax.axis_size("expert")
    route = [
        (i * blocks + j, (i + distance) * blocks + (j ^ 1))
        for i in range(sections)
        if 0 <= i + distance < sections
        for j in range(blocks)
    ]
    return lax.ppermute(block, ("pipe", "expert"), route)


def route_weights(routes, gates, experts, m):
    tokens = routes.shape[0]
    column = jnp.arange(experts * 2 * CAPACITY, dtype=jnp.int32)
    matches = routes[:, :, None] == column // (2 * CAPACITY)
    is_routed = jnp.any(matches, axis=1)
    earlier = jnp.tril(jnp.ones((tokens, tokens), jnp.bfloat16), -1)
    rank = jnp.dot(earlier, is_routed.astype(jnp.bfloat16), preferred_element_type=jnp.float32)
    gate_sum = jnp.sum(jnp.where(matches, gates[:, :, None], 0.0), axis=1)
    slot = column % (2 * CAPACITY) - m * CAPACITY
    chosen = is_routed & (rank == slot.astype(jnp.float32)) & (slot >= 0)
    return jnp.where(chosen, gate_sum, 0.0)


def on_diagonal(size):
    return lax.broadcasted_iota(jnp.int32, (size, size), 0) == lax.broadcasted_iota(jnp.int32, (size, size), 1)


def combine_kernel(received_ref, side0_ref, side1_ref, rows_ref, squares_ref):
    slots, columns = received_ref.shape
    tokens = side0_ref.shape[0]
    sides = (side0_ref, side1_ref)
    weights = [side[:, start : start + slots] for side in sides for start in (columns, columns + slots)]
    products = jnp.dot(jnp.concatenate(weights, axis=0), received_ref[...], preferred_element_type=jnp.float32)
    for m, side in enumerate(sides):
        high, low = (products[part * tokens : (part + 1) * tokens] for part in (2 * m, 2 * m + 1))
        layer_out = (side[:, :columns].astype(jnp.float32) + (high + low)).astype(jnp.bfloat16)
        rows_ref[m] = layer_out
        floats = layer_out.astype(jnp.float32)
        total = jnp.sum(floats * floats, axis=1, keepdims=True)
        squares_ref[m : m + 1] = jnp.sum(jnp.where(on_diagonal(tokens), total, 0.0), axis=0, keepdims=True)


def combine(received, sides, tokens):
    slots, columns = received.shape
    return pl.pallas_call(
        combine_kernel,
        out_shape=(
            jax.ShapeDtypeStruct((2, tokens, columns), jnp.bfloat16),
            jax.ShapeDtypeStruct((2, tokens), jnp.float32),
        ),
        cost_estimate=pl.CostEstimate(
            flops=8 * tokens * slots * columns, bytes_accessed=2 * slots * columns, transcendentals=0
        ),
        compiler_params=pltpu.CompilerParams(vmem_limit_bytes=8 << 20),
    )(received, *sides)


def norm_kernel(rows_ref, totals_ref, gains_ref, stream_ref, normed_ref):
    tokens, columns = rows_ref.shape[1:]
    totals = jnp.sum(totals_ref[...], axis=0)
    for m in range(2):
        total = jnp.sum(jnp.where(on_diagonal(tokens), totals[m : m + 1], 0.0), axis=1, keepdims=True)
        factor = lax.rsqrt(total / D + EPSILON)
        normed = rows_ref[m].astype(jnp.float32) * factor * gains_ref[m : m + 1]
        stream_ref[0, m] = rows_ref[m]
        normed_ref[0, m] = normed.astype(jnp.bfloat16)


def normalize(rows, totals, gains):
    shape = jax.ShapeDtypeStruct((1, *rows.shape), jnp.bfloat16)
    return pl.pallas_call(
        norm_kernel,
        out_shape=(shape, shape),
        cost_estimate=pl.CostEstimate(flops=4 * rows.size, bytes_accessed=4 * rows.size, transcendentals=0),
        compiler_params=pltpu.CompilerParams(vmem_limit_bytes=8 << 20),
    )(rows, totals, gains)


def per_device(stream, routes, gates, expert_hidden, down_weight, norm_gain):
    blocks = lax.axis_size("expert")
    experts = blocks // 2
    parity = lax.axis_index("expert") % 2
    section = lax.axis_index("pipe")
    sections = lax.axis_size("pipe")
    tokens, columns = stream.shape[2:]
    halves = [[j for j in range(blocks) if j % 2 == q] for q in range(2)]
    hidden = expert_hidden[0].reshape(2, experts, 2, CAPACITY, -1)
    kept = lax.dynamic_index_in_dim(hidden, parity, 2, keepdims=False).reshape(2, experts * CAPACITY, -1)
    sent = lax.dynamic_index_in_dim(hidden, 1 - parity, 2, keepdims=False).reshape(2, experts * CAPACITY, -1)

    kept, sent = lax.optimization_barrier((kept, sent))

    def project(rows):
        return jnp.dot(rows, down_weight[0], preferred_element_type=jnp.float32).astype(jnp.bfloat16)

    sums = []
    for m, distance in enumerate((1, -1)):
        theirs = shifted_to_partner(project(sent[m]), distance)
        own = shifted(project(kept[m]), distance)
        total = (theirs.astype(jnp.float32) + own.astype(jnp.float32)).astype(jnp.bfloat16)
        sums.append(total.reshape(experts, CAPACITY, columns))
    exchanged = lax.all_to_all(
        jnp.stack(sums, axis=1), "expert", 0, 0, axis_index_groups=halves, tiled=True
    )
    sides = []
    for m, distance in enumerate((1, -1)):
        weights = route_weights(routes[0, m], gates[0, m], experts, m)
        high = weights.astype(jnp.bfloat16)
        low = (weights - high.astype(jnp.float32)).astype(jnp.bfloat16)
        sides.append(shifted(jnp.concatenate([stream[0, m], high, low], axis=1), distance))
    received = exchanged.reshape(experts * 2 * CAPACITY, columns)
    rows, squares = combine(received, sides, tokens)
    totals = lax.all_gather(squares, "dp")
    gains = jnp.stack(
        [
            lax.dynamic_index_in_dim(norm_gain, jnp.clip(section - distance, 0, sections - 1), 0, keepdims=False)
            for distance in (1, -1)
        ]
    )
    return normalize(rows, totals, gains)


def solution(mesh):
    in_specs = (
        P("pipe", None, "expert", "dp"),
        P("pipe", None, "expert", None),
        P("pipe", None, "expert", None),
        P("pipe", None, None, "expert"),
        P("pipe", "expert", "dp"),
        P(None, "dp"),
    )
    out_specs = (P("pipe", None, "expert", "dp"), P("pipe", None, "expert", "dp"))
    return jax.shard_map(
        per_device, mesh=mesh, in_specs=in_specs, out_specs=out_specs, check_vma=False
    )
```

```python
import jax
import jax.numpy as jnp
from jax import lax
from jax.experimental import pallas as pl
from jax.experimental.pallas import tpu as pltpu
from jax.sharding import PartitionSpec as P

D = 7168
EPSILON = 1e-06
CAPACITY = 8


def shifted(block, distance):
    sections = range(lax.axis_size("pipe"))
    route = [(i - distance, i) for i in sections if i - distance in sections]
    return lax.ppermute(block, "pipe", route)


def shifted_to_partner(block, distance):
    sections, blocks = lax.axis_size("pipe"), lax.axis_size("expert")
    route = [
        (i * blocks + j, (i + distance) * blocks + (j ^ 1))
        for i in range(sections)
        if 0 <= i + distance < sections
        for j in range(blocks)
    ]
    return lax.ppermute(block, ("pipe", "expert"), route)


def route_weights(routes, gates, experts, m):
    tokens = routes.shape[0]
    column = jnp.arange(experts * 2 * CAPACITY, dtype=jnp.int32)
    matches = routes[:, :, None] == column // (2 * CAPACITY)
    is_routed = jnp.any(matches, axis=1)
    earlier = jnp.tril(jnp.ones((tokens, tokens), jnp.bfloat16), -1)
    rank = jnp.dot(earlier, is_routed.astype(jnp.bfloat16), preferred_element_type=jnp.float32)
    gate_sum = jnp.sum(jnp.where(matches, gates[:, :, None], 0.0), axis=1)
    slot = column % (2 * CAPACITY) - m * CAPACITY
    chosen = is_routed & (rank == slot.astype(jnp.float32)) & (slot >= 0)
    return jnp.where(chosen, gate_sum, 0.0)


def on_diagonal(size):
    return lax.broadcasted_iota(jnp.int32, (size, size), 0) == lax.broadcasted_iota(jnp.int32, (size, size), 1)


def combine_kernel(received_ref, side0_ref, side1_ref, rows_ref, squares_ref):
    slots, columns = received_ref.shape
    tokens = side0_ref.shape[0]
    sides = (side0_ref, side1_ref)
    weights = [side[:, start : start + slots] for side in sides for start in (columns, columns + slots)]
    products = jnp.dot(jnp.concatenate(weights, axis=0), received_ref[...], preferred_element_type=jnp.float32)
    for m, side in enumerate(sides):
        high, low = (products[part * tokens : (part + 1) * tokens] for part in (2 * m, 2 * m + 1))
        layer_out = (side[:, :columns].astype(jnp.float32) + (high + low)).astype(jnp.bfloat16)
        rows_ref[m] = layer_out
        floats = layer_out.astype(jnp.float32)
        total = jnp.sum(floats * floats, axis=1, keepdims=True)
        squares_ref[m : m + 1] = jnp.sum(jnp.where(on_diagonal(tokens), total, 0.0), axis=0, keepdims=True)


def combine(received, sides, tokens):
    slots, columns = received.shape
    return pl.pallas_call(
        combine_kernel,
        out_shape=(
            jax.ShapeDtypeStruct((2, tokens, columns), jnp.bfloat16),
            jax.ShapeDtypeStruct((2, tokens), jnp.float32),
        ),
        cost_estimate=pl.CostEstimate(
            flops=8 * tokens * slots * columns, bytes_accessed=2 * slots * columns, transcendentals=0
        ),
        compiler_params=pltpu.CompilerParams(vmem_limit_bytes=8 << 20),
    )(received, *sides)


def norm_kernel(rows_ref, totals_ref, gains_ref, stream_ref, normed_ref):
    m = pl.program_id(0)
    tokens = rows_ref.shape[1]
    totals = jnp.sum(totals_ref[...], axis=0)
    own = jnp.where(m == 0, totals[:1], totals[1:])
    gain = jnp.where(m == 0, gains_ref[:1], gains_ref[1:])
    total = jnp.sum(jnp.where(on_diagonal(tokens), own, 0.0), axis=1, keepdims=True)
    factor = lax.rsqrt(total / D + EPSILON)
    rows = rows_ref[0]
    stream_ref[0, 0] = rows
    normed_ref[0, 0] = (rows.astype(jnp.float32) * factor * gain).astype(jnp.bfloat16)


def normalize(rows, totals, gains):
    shape = jax.ShapeDtypeStruct((1, *rows.shape), jnp.bfloat16)
    out = pl.BlockSpec((1, 1, *rows.shape[1:]), lambda m: (0, m, 0, 0))
    return pl.pallas_call(
        norm_kernel,
        grid=(2,),
        in_specs=[
            pl.BlockSpec((1, *rows.shape[1:]), lambda m: (m, 0, 0)),
            pl.BlockSpec(totals.shape, lambda m: (0, 0, 0)),
            pl.BlockSpec(gains.shape, lambda m: (0, 0)),
        ],
        out_specs=(out, out),
        out_shape=(shape, shape),
        cost_estimate=pl.CostEstimate(flops=4 * rows.size, bytes_accessed=4 * rows.size, transcendentals=0),
        compiler_params=pltpu.CompilerParams(vmem_limit_bytes=8 << 20),
    )(rows, totals, gains)


def per_device(stream, routes, gates, expert_hidden, down_weight, norm_gain):
    blocks = lax.axis_size("expert")
    experts = blocks // 2
    parity = lax.axis_index("expert") % 2
    section = lax.axis_index("pipe")
    sections = lax.axis_size("pipe")
    tokens, columns = stream.shape[2:]
    halves = [[j for j in range(blocks) if j % 2 == q] for q in range(2)]
    hidden = expert_hidden[0].reshape(2, experts, 2, CAPACITY, -1)
    kept = lax.dynamic_index_in_dim(hidden, parity, 2, keepdims=False).reshape(2, experts * CAPACITY, -1)
    sent = lax.dynamic_index_in_dim(hidden, 1 - parity, 2, keepdims=False).reshape(2, experts * CAPACITY, -1)

    kept, sent = lax.optimization_barrier((kept, sent))

    def project(rows):
        return jnp.dot(rows, down_weight[0], preferred_element_type=jnp.float32).astype(jnp.bfloat16)

    rows = None
    for m, distance in enumerate((1, -1)):
        theirs = shifted_to_partner(project(sent[m]), distance)
        own = shifted(project(kept[m]), distance)
        total = (theirs.astype(jnp.float32) + own.astype(jnp.float32)).astype(jnp.bfloat16)
        total = total.reshape(experts, 1, CAPACITY, columns)
        if rows is None:
            rows = lax.optimization_barrier(jnp.concatenate([total, total], axis=1))
        else:
            rows = lax.dynamic_update_slice(rows, total, (0, m, 0, 0))
    exchanged = lax.all_to_all(rows, "expert", 0, 0, axis_index_groups=halves, tiled=True)
    sides = []
    for m, distance in enumerate((1, -1)):
        weights = route_weights(routes[0, m], gates[0, m], experts, m)
        high = weights.astype(jnp.bfloat16)
        low = (weights - high.astype(jnp.float32)).astype(jnp.bfloat16)
        sides.append(shifted(jnp.concatenate([stream[0, m], high, low], axis=1), distance))
    received = exchanged.reshape(experts * 2 * CAPACITY, columns)
    rows, squares = combine(received, sides, tokens)
    totals = lax.all_gather(squares, "dp")
    gains = jnp.stack(
        [
            lax.dynamic_index_in_dim(norm_gain, jnp.clip(section - distance, 0, sections - 1), 0, keepdims=False)
            for distance in (1, -1)
        ]
    )
    return normalize(rows, totals, gains)


def solution(mesh):
    in_specs = (
        P("pipe", None, "expert", "dp"),
        P("pipe", None, "expert", None),
        P("pipe", None, "expert", None),
        P("pipe", None, None, "expert"),
        P("pipe", "expert", "dp"),
        P(None, "dp"),
    )
    out_specs = (P("pipe", None, "expert", "dp"), P("pipe", None, "expert", "dp"))
    return jax.shard_map(
        per_device, mesh=mesh, in_specs=in_specs, out_specs=out_specs, check_vma=False
    )
```

```python
import jax
import jax.numpy as jnp
from jax import lax
from jax.experimental import pallas as pl
from jax.experimental.pallas import tpu as pltpu
from jax.sharding import PartitionSpec as P

D = 7168
EPSILON = 1e-06
CAPACITY = 8


def shifted(block, distance):
    sections = range(lax.axis_size("pipe"))
    route = [(i - distance, i) for i in sections if i - distance in sections]
    return lax.ppermute(block, "pipe", route)


def shifted_to_partner(block, distance):
    sections, blocks = lax.axis_size("pipe"), lax.axis_size("expert")
    route = [
        (i * blocks + j, (i + distance) * blocks + (j ^ 1))
        for i in range(sections)
        if 0 <= i + distance < sections
        for j in range(blocks)
    ]
    return lax.ppermute(block, ("pipe", "expert"), route)


def route_weights(routes, gates, experts, m):
    tokens = routes.shape[0]
    column = jnp.arange(experts * 2 * CAPACITY, dtype=jnp.int32)
    matches = routes[:, :, None] == column // (2 * CAPACITY)
    is_routed = jnp.any(matches, axis=1)
    earlier = jnp.tril(jnp.ones((tokens, tokens), jnp.bfloat16), -1)
    rank = jnp.dot(earlier, is_routed.astype(jnp.bfloat16), preferred_element_type=jnp.float32)
    gate_sum = jnp.sum(jnp.where(matches, gates[:, :, None], 0.0), axis=1)
    slot = column % (2 * CAPACITY) - m * CAPACITY
    chosen = is_routed & (rank == slot.astype(jnp.float32)) & (slot >= 0)
    return jnp.where(chosen, gate_sum, 0.0)


def on_diagonal(size):
    return lax.broadcasted_iota(jnp.int32, (size, size), 0) == lax.broadcasted_iota(jnp.int32, (size, size), 1)


def combine_kernel(received_ref, side0_ref, side1_ref, rows_ref, squares_ref):
    slots, columns = received_ref.shape
    tokens = side0_ref.shape[0]
    sides = (side0_ref, side1_ref)
    weights = [side[:, start : start + slots] for side in sides for start in (columns, columns + slots)]
    products = jnp.dot(jnp.concatenate(weights, axis=0), received_ref[...], preferred_element_type=jnp.float32)
    for m, side in enumerate(sides):
        high, low = (products[part * tokens : (part + 1) * tokens] for part in (2 * m, 2 * m + 1))
        layer_out = (side[:, :columns].astype(jnp.float32) + (high + low)).astype(jnp.bfloat16)
        rows_ref[m] = layer_out
        floats = layer_out.astype(jnp.float32)
        total = jnp.sum(floats * floats, axis=1, keepdims=True)
        squares_ref[m : m + 1] = jnp.sum(jnp.where(on_diagonal(tokens), total, 0.0), axis=0, keepdims=True)


def combine(received, sides, tokens):
    slots, columns = received.shape
    return pl.pallas_call(
        combine_kernel,
        out_shape=(
            jax.ShapeDtypeStruct((2, tokens, columns), jnp.bfloat16),
            jax.ShapeDtypeStruct((2, tokens), jnp.float32),
        ),
        cost_estimate=pl.CostEstimate(
            flops=8 * tokens * slots * columns, bytes_accessed=2 * slots * columns, transcendentals=0
        ),
        compiler_params=pltpu.CompilerParams(vmem_limit_bytes=8 << 20),
    )(received, *sides)


def norm_kernel(rows_ref, totals_ref, gains_ref, stream_ref, normed_ref):
    tokens, columns = rows_ref.shape[1:]
    totals = jnp.sum(totals_ref[...], axis=0)
    for m in range(2):
        total = jnp.sum(jnp.where(on_diagonal(tokens), totals[m : m + 1], 0.0), axis=1, keepdims=True)
        factor = lax.rsqrt(total / D + EPSILON)
        normed = rows_ref[m].astype(jnp.float32) * factor * gains_ref[m : m + 1]
        stream_ref[0, m] = rows_ref[m]
        normed_ref[0, m] = normed.astype(jnp.bfloat16)


def normalize(rows, totals, gains):
    shape = jax.ShapeDtypeStruct((1, *rows.shape), jnp.bfloat16)
    return pl.pallas_call(
        norm_kernel,
        out_shape=(shape, shape),
        cost_estimate=pl.CostEstimate(flops=4 * rows.size, bytes_accessed=4 * rows.size, transcendentals=0),
        compiler_params=pltpu.CompilerParams(vmem_limit_bytes=8 << 20),
    )(rows, totals, gains)


def per_device(stream, routes, gates, expert_hidden, down_weight, norm_gain):
    blocks = lax.axis_size("expert")
    experts = blocks // 2
    parity = lax.axis_index("expert") % 2
    section = lax.axis_index("pipe")
    sections = lax.axis_size("pipe")
    tokens, columns = stream.shape[2:]
    halves = [[j for j in range(blocks) if j % 2 == q] for q in range(2)]
    hidden = expert_hidden[0].reshape(2, experts, 2, CAPACITY, -1)
    kept = lax.dynamic_index_in_dim(hidden, parity, 2, keepdims=False).reshape(2, experts * CAPACITY, -1)
    sent = lax.dynamic_index_in_dim(hidden, 1 - parity, 2, keepdims=False).reshape(2, experts * CAPACITY, -1)

    kept, sent = lax.optimization_barrier((kept, sent))

    def project(rows):
        return jnp.dot(rows, down_weight[0], preferred_element_type=jnp.float32).astype(jnp.bfloat16)

    rows = None
    for m, distance in enumerate((1, -1)):
        theirs = shifted_to_partner(project(sent[m]), distance)
        own = shifted(project(kept[m]), distance)
        total = (theirs.astype(jnp.float32) + own.astype(jnp.float32)).astype(jnp.bfloat16)
        total = total.reshape(experts, 1, CAPACITY, columns)
        if rows is None:
            rows = lax.optimization_barrier(jnp.concatenate([total, total], axis=1))
        else:
            rows = lax.dynamic_update_slice(rows, total, (0, m, 0, 0))
    exchanged = lax.all_to_all(rows, "expert", 0, 0, axis_index_groups=halves, tiled=True)
    sides = []
    for m, distance in enumerate((1, -1)):
        weights = route_weights(routes[0, m], gates[0, m], experts, m)
        high = weights.astype(jnp.bfloat16)
        low = (weights - high.astype(jnp.float32)).astype(jnp.bfloat16)
        sides.append(shifted(jnp.concatenate([stream[0, m], high, low], axis=1), distance))
    received = exchanged.reshape(experts * 2 * CAPACITY, columns)
    rows, squares = combine(received, sides, tokens)
    totals = lax.all_gather(squares, "dp")
    gains = jnp.stack(
        [
            lax.dynamic_index_in_dim(norm_gain, jnp.clip(section - distance, 0, sections - 1), 0, keepdims=False)
            for distance in (1, -1)
        ]
    )
    return normalize(rows, totals, gains)


def solution(mesh):
    in_specs = (
        P("pipe", None, "expert", "dp"),
        P("pipe", None, "expert", None),
        P("pipe", None, "expert", None),
        P("pipe", None, None, "expert"),
        P("pipe", "expert", "dp"),
        P(None, "dp"),
    )
    out_specs = (P("pipe", None, "expert", "dp"), P("pipe", None, "expert", "dp"))
    return jax.shard_map(
        per_device, mesh=mesh, in_specs=in_specs, out_specs=out_specs, check_vma=False
    )
```

```python
import jax
import jax.numpy as jnp
from jax import lax
from jax.experimental import pallas as pl
from jax.experimental.pallas import tpu as pltpu
from jax.sharding import PartitionSpec as P

D = 7168
EPSILON = 1e-06
CAPACITY = 8


def shifted(block, distance):
    sections = range(lax.axis_size("pipe"))
    route = [(i - distance, i) for i in sections if i - distance in sections]
    return lax.ppermute(block, "pipe", route)


def shifted_to_partner(block, distance):
    sections, blocks = lax.axis_size("pipe"), lax.axis_size("expert")
    route = [
        (i * blocks + j, (i + distance) * blocks + (j ^ 1))
        for i in range(sections)
        if 0 <= i + distance < sections
        for j in range(blocks)
    ]
    return lax.ppermute(block, ("pipe", "expert"), route)


def route_weights(routes, gates, experts, m):
    tokens = routes.shape[0]
    column = jnp.arange(experts * 2 * CAPACITY, dtype=jnp.int32)
    matches = routes[:, :, None] == column // (2 * CAPACITY)
    is_routed = jnp.any(matches, axis=1)
    earlier = jnp.tril(jnp.ones((tokens, tokens), jnp.bfloat16), -1)
    rank = jnp.dot(earlier, is_routed.astype(jnp.bfloat16), preferred_element_type=jnp.float32)
    gate_sum = jnp.sum(jnp.where(matches, gates[:, :, None], 0.0), axis=1)
    slot = column % (2 * CAPACITY) - m * CAPACITY
    chosen = is_routed & (rank == slot.astype(jnp.float32)) & (slot >= 0)
    return jnp.where(chosen, gate_sum, 0.0)


def on_diagonal(size):
    return lax.broadcasted_iota(jnp.int32, (size, size), 0) == lax.broadcasted_iota(jnp.int32, (size, size), 1)


def combine_kernel(received_ref, side0_ref, side1_ref, rows_ref, squares_ref):
    slots, columns = received_ref.shape
    tokens = side0_ref.shape[0]
    sides = (side0_ref, side1_ref)
    weights = [side[:, start : start + slots] for side in sides for start in (columns, columns + slots)]
    products = jnp.dot(jnp.concatenate(weights, axis=0), received_ref[...], preferred_element_type=jnp.float32)
    for m, side in enumerate(sides):
        high, low = (products[part * tokens : (part + 1) * tokens] for part in (2 * m, 2 * m + 1))
        layer_out = (side[:, :columns].astype(jnp.float32) + (high + low)).astype(jnp.bfloat16)
        rows_ref[m] = layer_out
        floats = layer_out.astype(jnp.float32)
        total = jnp.sum(floats * floats, axis=1, keepdims=True)
        squares_ref[m : m + 1] = jnp.sum(jnp.where(on_diagonal(tokens), total, 0.0), axis=0, keepdims=True)


def combine(received, sides, tokens):
    slots, columns = received.shape
    return pl.pallas_call(
        combine_kernel,
        out_shape=(
            jax.ShapeDtypeStruct((2, tokens, columns), jnp.bfloat16),
            jax.ShapeDtypeStruct((2, tokens), jnp.float32),
        ),
        cost_estimate=pl.CostEstimate(
            flops=8 * tokens * slots * columns, bytes_accessed=2 * slots * columns, transcendentals=0
        ),
        compiler_params=pltpu.CompilerParams(vmem_limit_bytes=8 << 20),
    )(received, *sides)


def norm_kernel(rows_ref, totals_ref, gains_ref, stream_ref, normed_ref):
    tokens, columns = rows_ref.shape[1:]
    totals = jnp.sum(totals_ref[...], axis=0)
    for m in range(2):
        total = jnp.sum(jnp.where(on_diagonal(tokens), totals[m : m + 1], 0.0), axis=1, keepdims=True)
        factor = lax.rsqrt(total / D + EPSILON)
        normed = rows_ref[m].astype(jnp.float32) * factor * gains_ref[m : m + 1]
        stream_ref[0, m] = rows_ref[m]
        normed_ref[0, m] = normed.astype(jnp.bfloat16)


def normalize(rows, totals, gains):
    shape = jax.ShapeDtypeStruct((1, *rows.shape), jnp.bfloat16)
    return pl.pallas_call(
        norm_kernel,
        out_shape=(shape, shape),
        cost_estimate=pl.CostEstimate(flops=4 * rows.size, bytes_accessed=4 * rows.size, transcendentals=0),
        compiler_params=pltpu.CompilerParams(vmem_limit_bytes=8 << 20),
    )(rows, totals, gains)


def per_device(stream, routes, gates, expert_hidden, down_weight, norm_gain):
    blocks = lax.axis_size("expert")
    experts = blocks // 2
    parity = lax.axis_index("expert") % 2
    section = lax.axis_index("pipe")
    sections = lax.axis_size("pipe")
    tokens, columns = stream.shape[2:]
    halves = [[j for j in range(blocks) if j % 2 == q] for q in range(2)]
    hidden = expert_hidden[0].reshape(2, experts, 2, CAPACITY, -1)
    kept = lax.dynamic_index_in_dim(hidden, parity, 2, keepdims=False).reshape(2, experts * CAPACITY, -1)
    sent = lax.dynamic_index_in_dim(hidden, 1 - parity, 2, keepdims=False).reshape(2, experts * CAPACITY, -1)

    kept, sent = lax.optimization_barrier((kept, sent))

    def project(rows):
        return jnp.dot(rows, down_weight[0], preferred_element_type=jnp.float32).astype(jnp.bfloat16)

    rows = None
    for m, distance in ((1, -1), (0, 1)):
        theirs = shifted_to_partner(project(sent[m]), distance)
        own = shifted(project(kept[m]), distance)
        total = (theirs.astype(jnp.float32) + own.astype(jnp.float32)).astype(jnp.bfloat16)
        total = total.reshape(experts, 1, CAPACITY, columns)
        if rows is None:
            rows = lax.optimization_barrier(jnp.concatenate([total, total], axis=1))
        else:
            rows = lax.dynamic_update_slice(rows, total, (0, m, 0, 0))
    exchanged = lax.all_to_all(rows, "expert", 0, 0, axis_index_groups=halves, tiled=True)
    sides = []
    for m, distance in enumerate((1, -1)):
        weights = route_weights(routes[0, m], gates[0, m], experts, m)
        high = weights.astype(jnp.bfloat16)
        low = (weights - high.astype(jnp.float32)).astype(jnp.bfloat16)
        sides.append(shifted(jnp.concatenate([stream[0, m], high, low], axis=1), distance))
    received = exchanged.reshape(experts * 2 * CAPACITY, columns)
    rows, squares = combine(received, sides, tokens)
    totals = lax.all_gather(squares, "dp")
    gains = jnp.stack(
        [
            lax.dynamic_index_in_dim(norm_gain, jnp.clip(section - distance, 0, sections - 1), 0, keepdims=False)
            for distance in (1, -1)
        ]
    )
    return normalize(rows, totals, gains)


def solution(mesh):
    in_specs = (
        P("pipe", None, "expert", "dp"),
        P("pipe", None, "expert", None),
        P("pipe", None, "expert", None),
        P("pipe", None, None, "expert"),
        P("pipe", "expert", "dp"),
        P(None, "dp"),
    )
    out_specs = (P("pipe", None, "expert", "dp"), P("pipe", None, "expert", "dp"))
    return jax.shard_map(
        per_device, mesh=mesh, in_specs=in_specs, out_specs=out_specs, check_vma=False
    )
```
